32 devices in a mesh: group: 4 (over x, core), inner: 8 (over z, y).
Axes of the slice: x: 2, y: 2, z: 4, core: 2. Of those that a mesh axis runs over, the one named last changes fastest.
Arguments:
- x_self: bfloat16 [32768, 256], P(('group', 'inner')), may hold values from -6 to 6
- x_agg: bfloat16 [32768, 256], P(('group', 'inner')), may hold values from -6 to 6
- w_self: bfloat16 [256, 256], replicated, may hold values from -0.25 to 0.25
- w_nbr: bfloat16 [256, 256], replicated, may hold values from -0.25 to 0.25
- b_layer: float32 [256], replicated, may hold values from -3 to 3
- w_one: bfloat16 [256, 512], replicated, may hold values from -0.375 to 0.375
- b_one: float32 [512], replicated, may hold values from -3 to 3
- w_two: bfloat16 [512, 512], replicated, may hold values from -0.25 to 0.25
- b_two: float32 [512], replicated, may hold values from -3 to 3
- w_out: float32 [512], replicated, may hold values from -2 to 2
- send_lists: int32 [128, 8, 96], P(('group', 'inner')), may hold values from 0 to 1023, as said below
- endpoint_slots: int32 [16384, 2], P(('group', 'inner')), may hold values from 0 to 3071, as said below
- neg_index: int32 [16384, 4], P(('group', 'inner')), may hold values from 0 to 511, as said below
Outputs:
- grad_self: bfloat16 [32768, 256], P(('group', 'inner'))
- grad_agg: bfloat16 [32768, 256], P(('group', 'inner'))
- grad_scorer: float32 [393216], P(('group', 'inner'))
- grad_layer: float32 [131072], P(('group', 'inner'))
- grad_bias: float32 [1792], replicated
The draws below stay inside these ranges and needn't reach their ends.
Inputs may be any that keep to these rules, and one draw needn't show every extreme that they name: `send_lists`: viewed as [32, 32, 96] (owner, requesting device, slot), each entry is a row of the owner's block of 1024 nodes, and the 96 entries of one owner and one requesting device are distinct. Slots that endpoint_slots never names hold arbitrary rows. `endpoint_slots`: each entry of device r's block is a slot o * 96 + c of that device and names the node of send_lists' entry (o, r, c). `neg_index`: entry [p, k] is the index, within the same block of 512 positives, of another positive whose destination serves as the k-th negative of p; it is never p itself.
All inputs are finite; a program needn't handle non-finite values.
Results may differ from the reference program's by a relative error of at most 0.0075.
Values may be sent and summed in bfloat16 or wider, within the bound.
A program may use at most 128 MiB of HBM per device.

```python
import jax
import jax.numpy as jnp
from jax import lax

F = 256
H = 512
POS_DEV = 512
NEG = 4
OWNERS = 32
NODE_DEV = 1024
NODES = 32768
POSITIVES = 16384
CAP = 96
PAIRS_DEV = 2560
N_GROUP = 4


def plan_counts(key):
    mean_slots = 2 * POS_DEV // OWNERS
    shuffled = jax.random.permutation(jax.random.fold_in(key, 11), OWNERS)
    owner_ids = jnp.arange(OWNERS, dtype=jnp.int32)
    hub_owner = jnp.logical_or(shuffled < max(OWNERS // 16, 1) - 1, owner_ids == OWNERS - 1)
    drawn = jax.random.randint(jax.random.fold_in(key, 12), (OWNERS, OWNERS), 1, 2 * mean_slots)
    counts = jnp.where(hub_owner[None, :], CAP, drawn).astype(jnp.int32)
    return (counts, hub_owner)


def draw_send_lists(key, part):
    counts, hub_owner = plan_counts(key)
    spread_start = jax.random.randint(jax.random.fold_in(key, 21), (OWNERS, OWNERS), 0, NODE_DEV)
    hot_start = jax.random.randint(jax.random.fold_in(key, 22), (OWNERS, OWNERS), 0, NODE_DEV // 8)
    hot_start = hot_start.at[OWNERS - 1, 0].set(NODE_DEV - CAP).at[OWNERS - 1, 1].set(0)
    stride = NODE_DEV // CAP
    slot_ids = jnp.arange(CAP, dtype=jnp.int32)
    spread_rows = (spread_start[:, :, None] + slot_ids * stride) % NODE_DEV
    packed_rows = hot_start[:, :, None] + slot_ids
    row_ids = jnp.where(hub_owner[:, None, None], packed_rows, spread_rows)
    return row_ids.reshape(OWNERS * N_GROUP, OWNERS // N_GROUP, CAP).astype(jnp.int32)


def draw_endpoint_slots(key, part):
    counts, hub_owner = plan_counts(key)
    cum_counts = jnp.cumsum(counts, axis=1)
    live_slots = cum_counts[:, -1]
    chosen = jax.random.randint(jax.random.fold_in(key, 31), (OWNERS, POS_DEV * 2), 0, live_slots[:, None])
    chosen = chosen.at[:, 0].set(live_slots - 1).at[:, 1].set(0)
    owner_ids = jax.vmap(lambda edges, picks: jnp.searchsorted(edges, picks, side='right'))(cum_counts, chosen)
    owner_ids = owner_ids.astype(jnp.int32)
    first_slot = cum_counts - counts
    offset = chosen - jnp.take_along_axis(first_slot, owner_ids, axis=1)
    slot_ids = owner_ids * CAP + offset
    return slot_ids.reshape(POSITIVES, 2).astype(jnp.int32)


def draw_neg_index(key, part):
    positions = jnp.arange(POS_DEV, dtype=jnp.int32)[None, :, None]
    shift_by = jax.random.randint(jax.random.fold_in(key, 41), (OWNERS, POS_DEV, NEG), 1, POS_DEV)
    shift_by = shift_by.at[0, 0, 0].set(POS_DEV - 1).at[0, 1, 0].set(POS_DEV - 1)
    return ((positions + shift_by) % POS_DEV).reshape(POSITIVES, NEG).astype(jnp.int32)


def block_scale(key, shape, shards, least, high):
    loudness = 1.0
    for position, shards_of in shards:
        steps = jax.random.uniform(jax.random.fold_in(jax.random.fold_in(key, 6), position), (shards_of,), jnp.float32, least / len(shards), high / len(shards))
        loudness = loudness * jnp.repeat(jnp.exp(steps), shape[position] // shards_of).reshape((-1,) + (1,) * (len(shape) - 1 - position))
    return loudness


def centred(rng, extent, spread, reach, cuts=(), held_as=jnp.bfloat16):
    gain = block_scale(rng, extent, cuts, -0.22, 0.18) if cuts else 1.0
    result = jax.random.normal(rng, extent, jnp.float32) * spread * gain
    return jnp.minimum(jnp.maximum(result, -reach), reach).astype(held_as)


def setup_inputs(seed: int = 0) -> dict:
    streams_of = jax.random.split(jax.random.key(seed), 14)
    x_self = centred(streams_of[0], (NODES, F), 1.0, 6.0, ((0, 32),))
    x_agg = centred(streams_of[1], (NODES, F), 1.0, 6.0, ((0, 32),))
    w_self = centred(streams_of[2], (F, F), (2 * F) ** -0.5, 0.25)
    w_nbr = centred(streams_of[3], (F, F), (2 * F) ** -0.5, 0.25)
    b_layer = centred(streams_of[4], (F,), 0.5, 3.0, (), jnp.float32)
    w_one = centred(streams_of[5], (F, H), F ** -0.5, 0.375)
    b_one = centred(streams_of[6], (H,), 0.5, 3.0, (), jnp.float32)
    w_two = centred(streams_of[7], (H, H), H ** -0.5, 0.25)
    b_two = centred(streams_of[8], (H,), 0.5, 3.0, (), jnp.float32)
    w_out = centred(streams_of[9], (H,), 0.3, 2.0, (), jnp.float32)
    send_lists = draw_send_lists(jax.random.fold_in(streams_of[13], 71), 0)
    endpoint_slots = draw_endpoint_slots(jax.random.fold_in(streams_of[13], 71), 0)
    neg_index = draw_neg_index(jax.random.fold_in(streams_of[13], 71), 0)
    return dict(x_self=x_self, x_agg=x_agg, w_self=w_self, w_nbr=w_nbr, b_layer=b_layer, w_one=w_one, b_one=b_one, w_two=w_two, b_two=b_two, w_out=w_out, send_lists=send_lists, endpoint_slots=endpoint_slots, neg_index=neg_index)


def silu_slope(inputs):
    sigmoid_of = jax.nn.sigmoid(inputs)
    return sigmoid_of * (1.0 + inputs * (1.0 - sigmoid_of))


def dot_first(first_op, second_op):
    return lax.dot_general(first_op, second_op, (((0,), (0,)), ((), ())), preferred_element_type=jnp.float32)


def dot_last(first_op, second_op):
    return lax.dot_general(first_op, second_op, (((1,), (1,)), ((), ())), preferred_element_type=jnp.float32)


def reference(x_self, x_agg, w_self, w_nbr, b_layer, w_one, b_one, w_two, b_two, w_out, send_lists, endpoint_slots, neg_index):
    pre_act = jnp.dot(x_self, w_self, preferred_element_type=jnp.float32) + jnp.dot(x_agg, w_nbr, preferred_element_type=jnp.float32) + b_layer
    node_table = jax.nn.silu(pre_act).astype(jnp.bfloat16)
    lists = send_lists.reshape(OWNERS, OWNERS, CAP)
    slot_blocks = endpoint_slots.reshape(OWNERS, POS_DEV, 2)
    neg_blocks = neg_index.reshape(OWNERS, POS_DEV, NEG)
    labels = (jnp.arange(PAIRS_DEV, dtype=jnp.int32) < POS_DEV).astype(jnp.float32)

    def requester_step(carry, inputs):
        node_grads, grad_first, grad_second, bias_one, bias_two, bias_out = carry
        requester, slot_block, neg_block = inputs
        owner_ids = slot_block // CAP
        column = slot_block % CAP
        owner_rows = lists[owner_ids, requester, column]
        node_ids = (owner_ids * NODE_DEV + owner_rows).astype(jnp.int32)
        neg_flat = neg_block.T.reshape(-1)
        src_nodes = node_ids[:, 0]
        dst_nodes = node_ids[:, 1]
        left_nodes = jnp.tile(src_nodes, 1 + NEG)
        right_nodes = jnp.concatenate([dst_nodes, dst_nodes[neg_flat]])
        left_rows = node_table[left_nodes]
        right_rows = node_table[right_nodes]
        joint_rows = (left_rows.astype(jnp.float32) * right_rows.astype(jnp.float32)).astype(jnp.bfloat16)
        a_one = jnp.dot(joint_rows, w_one, preferred_element_type=jnp.float32) + b_one
        h_one = jax.nn.silu(a_one).astype(jnp.bfloat16)
        a_two = jnp.dot(h_one, w_two, preferred_element_type=jnp.float32) + b_two
        h_two = jax.nn.silu(a_two)
        scores = jnp.sum(h_two * w_out, axis=1)
        loss_slope = jax.nn.sigmoid(scores) - labels
        d_two = (loss_slope[:, None] * w_out) * silu_slope(a_two)
        d_two_low = d_two.astype(jnp.bfloat16)
        d_one = dot_last(d_two_low, w_two) * silu_slope(a_one)
        d_one_low = d_one.astype(jnp.bfloat16)
        d_joint = dot_last(d_one_low, w_one)
        d_left = d_joint * right_rows.astype(jnp.float32)
        d_right = d_joint * left_rows.astype(jnp.float32)
        node_grads = node_grads.at[left_nodes].add(d_left).at[right_nodes].add(d_right)
        grad_first = grad_first + dot_first(joint_rows, d_one_low)
        grad_second = grad_second + dot_first(h_one, d_two_low)
        bias_one = bias_one + jnp.sum(d_one, axis=0)
        bias_two = bias_two + jnp.sum(d_two, axis=0)
        bias_out = bias_out + jnp.sum(loss_slope[:, None] * h_two, axis=0)
        return (node_grads, grad_first, grad_second, bias_one, bias_two, bias_out), None

    initial = (jnp.zeros((NODES, F), jnp.float32), jnp.zeros((F, H), jnp.float32), jnp.zeros((H, H), jnp.float32),
               jnp.zeros((H,), jnp.float32), jnp.zeros((H,), jnp.float32), jnp.zeros((H,), jnp.float32))
    carried, unused = lax.scan(requester_step, initial, (jnp.arange(OWNERS, dtype=jnp.int32), slot_blocks, neg_blocks))
    node_grads, grad_first, grad_second, bias_one, bias_two, bias_out = carried
    d_pre = node_grads * silu_slope(pre_act)
    d_pre_low = d_pre.astype(jnp.bfloat16)
    grad_self = dot_last(d_pre_low, w_self).astype(jnp.bfloat16)
    grad_agg = dot_last(d_pre_low, w_nbr).astype(jnp.bfloat16)
    grad_scorer = jnp.concatenate([grad_first.reshape(-1), grad_second.reshape(-1)]) / PAIRS_DEV
    grad_layer = jnp.concatenate([dot_first(x_self, d_pre_low).reshape(-1), dot_first(x_agg, d_pre_low).reshape(-1)]) / PAIRS_DEV
    grad_bias = jnp.concatenate([bias_one, bias_two, bias_out, jnp.sum(d_pre, axis=0)]) / PAIRS_DEV
    return (grad_self, grad_agg, grad_scorer, grad_layer, grad_bias)
```

```python
import functools

import jax
import jax.numpy as jnp
from jax import lax
from jax.experimental import pallas as pl
from jax.experimental.pallas import tpu as pltpu
from jax.sharding import PartitionSpec as P

MESH = pl.DeviceIdType.MESH
VMEM = pltpu.VMEM
LOW = jnp.bfloat16


def silu_slope(inputs):
    sigmoid_of = jax.nn.sigmoid(inputs)
    return sigmoid_of * (1.0 + inputs * (1.0 - sigmoid_of))


def dot_first(first_op, second_op):
    return lax.dot_general(
        first_op, second_op, (((0,), (0,)), ((), ())), preferred_element_type=jnp.float32
    )


def dot_last(first_op, second_op):
    return lax.dot_general(
        first_op, second_op, (((1,), (1,)), ((), ())), preferred_element_type=jnp.float32
    )


def dot_plain(first_op, second_op):
    return jnp.dot(first_op, second_op, preferred_element_type=jnp.float32)


def place(groups, inners):
    group = lax.axis_index("group")
    inner = lax.axis_index("inner")
    return group, inner, group * inners + inner


def entry_barrier(groups, inners):
    owners = groups * inners
    _, _, me = place(groups, inners)
    barrier = pltpu.get_barrier_semaphore()

    def greet(step, carry):
        peer = lax.rem(me + step, owners)
        pl.semaphore_signal(
            barrier,
            inc=1,
            device_id=(peer // inners, lax.rem(peer, inners)),
            device_id_type=MESH,
        )
        return carry

    lax.fori_loop(1, owners, greet, 0)
    pl.semaphore_wait(barrier, owners - 1)


def exchange_copy(groups, inners, step, landing, src, dst, sends, recvs):
    owners = groups * inners
    _, _, me = place(groups, inners)
    peer = lax.rem(me + step, owners)
    slot = peer if landing else me
    return pltpu.make_async_remote_copy(
        src_ref=src.at[peer],
        dst_ref=dst.at[slot],
        send_sem=sends.at[peer],
        recv_sem=recvs.at[slot],
        device_id=(peer // inners, lax.rem(peer, inners)),
        device_id_type=MESH,
    )


def exchange_start(groups, inners, src, dst, own_sem, sends, recvs):
    _, _, me = place(groups, inners)
    pltpu.make_async_copy(src.at[me], dst.at[me], own_sem).start()

    def start(step, carry):
        exchange_copy(groups, inners, step, False, src, dst, sends, recvs).start()
        return carry

    lax.fori_loop(1, groups * inners, start, 0)


def exchange_wait(groups, inners, src, dst, own_sem, sends, recvs):
    _, _, me = place(groups, inners)
    pltpu.make_async_copy(src.at[me], dst.at[me], own_sem).wait()

    def finish(step, carry):
        copy = exchange_copy(groups, inners, step, True, src, dst, sends, recvs)
        copy.wait_send()
        copy.wait_recv()
        return carry

    lax.fori_loop(1, groups * inners, finish, 0)


def axis_copy(groups, inners, along, step, landing, src, dst, sends, recvs, whole):
    group, inner, _ = place(groups, inners)
    if along == "group":
        mine, peer = group, lax.rem(group + step, groups)
        device = (peer, inner)
    else:
        mine, peer = inner, lax.rem(inner + step, inners)
        device = (group, peer)
    slot = peer if landing else mine
    return pltpu.make_async_remote_copy(
        src_ref=src if whole else src.at[peer],
        dst_ref=dst.at[slot],
        send_sem=sends.at[peer],
        recv_sem=recvs.at[slot],
        device_id=device,
        device_id_type=MESH,
    )


def axis_start(groups, inners, along, src, dst, sends, recvs, whole=False):
    for step in range(1, groups if along == "group" else inners):
        axis_copy(
            groups, inners, along, step, False, src, dst, sends, recvs, whole
        ).start()


def axis_wait(groups, inners, along, src, dst, sends, recvs, whole=False):
    for step in range(1, groups if along == "group" else inners):
        copy = axis_copy(groups, inners, along, step, True, src, dst, sends, recvs, whole)
        copy.wait_send()
        copy.wait_recv()


def fetch_kernel(groups, inners, src, dst, own_sem, sends, recvs):
    entry_barrier(groups, inners)
    exchange_start(groups, inners, src, dst, own_sem, sends, recvs)
    exchange_wait(groups, inners, src, dst, own_sem, sends, recvs)


def share_middle(groups, inners, src, land_one, stage, land_two):
    group, inner, _ = place(groups, inners)
    land_one[group] = src[group]
    total = land_one[0].astype(jnp.float32)
    for index in range(1, groups):
        total = total + land_one[index].astype(jnp.float32)
    rows = total.shape[0] // inners
    for index in range(inners):
        stage[index] = total[index * rows : (index + 1) * rows]
    land_two[inner] = stage[inner]


def share_end(inners, land_two):
    total = land_two[0]
    for index in range(1, inners):
        total = total + land_two[index]
    return total


def return_kernel(
    groups,
    inners,
    src,
    terms,
    dst,
    share,
    land_one,
    stage,
    land_two,
    own_sem,
    sends,
    recvs,
    g_sends,
    g_recvs,
    i_sends,
    i_recvs,
):
    entry_barrier(groups, inners)
    axis_start(groups, inners, "group", terms, land_one, g_sends, g_recvs)
    exchange_start(groups, inners, src, dst, own_sem, sends, recvs)
    axis_wait(groups, inners, "group", terms, land_one, g_sends, g_recvs)
    share_middle(groups, inners, terms, land_one, stage, land_two)
    axis_start(groups, inners, "inner", stage, land_two, i_sends, i_recvs)
    axis_wait(groups, inners, "inner", stage, land_two, i_sends, i_recvs)
    share[...] = share_end(inners, land_two)
    exchange_wait(groups, inners, src, dst, own_sem, sends, recvs)


def layer_kernel(
    groups,
    inners,
    terms,
    bias,
    share,
    bias_out,
    land_one,
    stage,
    land_two,
    bias_one,
    bias_stage,
    bias_two,
    g_sends,
    g_recvs,
    i_sends,
    i_recvs,
    bg_sends,
    bg_recvs,
    bi_sends,
    bi_recvs,
):
    group, inner, _ = place(groups, inners)
    entry_barrier(groups, inners)
    axis_start(groups, inners, "group", terms, land_one, g_sends, g_recvs)
    axis_start(groups, inners, "group", bias, bias_one, bg_sends, bg_recvs, True)
    axis_wait(groups, inners, "group", terms, land_one, g_sends, g_recvs)
    share_middle(groups, inners, terms, land_one, stage, land_two)
    axis_start(groups, inners, "inner", stage, land_two, i_sends, i_recvs)
    axis_wait(groups, inners, "group", bias, bias_one, bg_sends, bg_recvs, True)
    bias_one[group] = bias[...]
    bias_stage[...] = share_end(groups, bias_one)
    bias_two[inner] = bias_stage[...]
    axis_start(groups, inners, "inner", bias_stage, bias_two, bi_sends, bi_recvs, True)
    axis_wait(groups, inners, "inner", stage, land_two, i_sends, i_recvs)
    share[...] = share_end(inners, land_two)
    axis_wait(groups, inners, "inner", bias_stage, bias_two, bi_sends, bi_recvs, True)
    bias_out[...] = share_end(inners, bias_two)


def in_vmem(count):
    return [pl.BlockSpec(memory_space=VMEM)] * count


def sems(count):
    return pltpu.SemaphoreType.DMA((count,))


def settings(index):
    return pltpu.CompilerParams(
        collective_id=index, has_side_effects=True, vmem_limit_bytes=24 * 1024 * 1024
    )


def fetch_rows(groups, inners, outgoing):
    owners = groups * inners
    return pl.pallas_call(
        functools.partial(fetch_kernel, groups, inners),
        out_shape=jax.ShapeDtypeStruct(outgoing.shape, outgoing.dtype),
        in_specs=in_vmem(1),
        out_specs=pl.BlockSpec(memory_space=VMEM),
        scratch_shapes=[pltpu.SemaphoreType.DMA, sems(owners), sems(owners)],
        compiler_params=settings(0),
        name="fetch_rows",
    )(outgoing)


def share_scratch(groups, inners, chunk, width):
    rows = chunk // inners
    return [
        VMEM((groups, chunk, width), LOW),
        VMEM((inners, rows, width), jnp.float32),
        VMEM((inners, rows, width), jnp.float32),
    ]


def return_rows(groups, inners, outbound, terms):
    owners = groups * inners
    chunk, width = terms.shape[0] // groups, terms.shape[1]
    return pl.pallas_call(
        functools.partial(return_kernel, groups, inners),
        out_shape=(
            jax.ShapeDtypeStruct(outbound.shape, outbound.dtype),
            jax.ShapeDtypeStruct((chunk // inners, width), jnp.float32),
        ),
        in_specs=in_vmem(2),
        out_specs=tuple(in_vmem(2)),
        scratch_shapes=share_scratch(groups, inners, chunk, width)
        + [
            pltpu.SemaphoreType.DMA,
            sems(owners),
            sems(owners),
            sems(groups),
            sems(groups),
            sems(inners),
            sems(inners),
        ],
        compiler_params=settings(1),
        name="return_rows",
    )(outbound, terms.reshape(groups, chunk, width))


def share_layer(groups, inners, terms, bias):
    chunk, width = terms.shape[0] // groups, terms.shape[1]
    length = bias.shape[0]
    lines = -(-length // 1024) * 8
    tall = jnp.pad(bias, (0, lines * 128 - length)).reshape(lines, 128)
    share, total = pl.pallas_call(
        functools.partial(layer_kernel, groups, inners),
        out_shape=(
            jax.ShapeDtypeStruct((chunk // inners, width), jnp.float32),
            jax.ShapeDtypeStruct((lines, 128), jnp.float32),
        ),
        in_specs=in_vmem(2),
        out_specs=tuple(in_vmem(2)),
        scratch_shapes=share_scratch(groups, inners, chunk, width)
        + [
            VMEM((groups, lines, 128), jnp.float32),
            VMEM((lines, 128), jnp.float32),
            VMEM((inners, lines, 128), jnp.float32),
        ]
        + [
            sems(groups),
            sems(groups),
            sems(inners),
            sems(inners),
            sems(groups),
            sems(groups),
            sems(inners),
            sems(inners),
        ],
        compiler_params=settings(2),
        name="share_layer",
    )(terms.reshape(groups, chunk, width), tall)
    return share.reshape(-1), total.reshape(-1)[:length]


def pick(ids, count):
    return (ids[:, None] == jnp.arange(count, dtype=jnp.int32)[None, :]).astype(LOW)


def pick_across(ids, count):
    return (jnp.arange(count, dtype=jnp.int32)[:, None] == ids[None, :]).astype(LOW)


def body(
    x_self,
    x_agg,
    w_self,
    w_nbr,
    b_layer,
    w_one,
    b_one,
    w_two,
    b_two,
    w_out,
    send_lists,
    endpoint_slots,
    neg_index,
):
    groups = lax.axis_size("group")
    inners = lax.axis_size("inner")
    owners = groups * inners
    nodes, width = x_self.shape
    pos_rows = endpoint_slots.shape[0]
    negatives = neg_index.shape[1]
    capacity = send_lists.shape[2]
    pairs_dev = pos_rows * (1 + negatives)
    padded = -(-capacity // 16) * 16
    slots = owners * padded
    lists = send_lists.reshape(owners, capacity)
    ends = endpoint_slots.T.reshape(-1)
    if padded != capacity:
        lists = jnp.pad(lists, ((0, 0), (0, padded - capacity)), constant_values=-1)
        ends = ends + (ends // capacity) * (padded - capacity)
    flat_lists = lists.reshape(-1)
    neg_flat = neg_index.T.reshape(-1)

    pre_act = dot_plain(x_self, w_self) + dot_plain(x_agg, w_nbr) + b_layer
    node_table = jax.nn.silu(pre_act).astype(LOW)
    outgoing = dot_plain(pick(flat_lists, nodes), node_table).astype(LOW)
    fetched = fetch_rows(groups, inners, outgoing.reshape(owners, padded, width))
    slot_rows = fetched.reshape(slots, width)
    end_rows = dot_plain(pick(ends, slots), slot_rows).astype(LOW)
    src_rows, dst_rows = end_rows[:pos_rows], end_rows[pos_rows:]
    neg_rows = dot_plain(pick(neg_flat, pos_rows), dst_rows).astype(LOW)
    right_rows = jnp.concatenate([dst_rows, neg_rows], axis=0)
    left_rows = jnp.tile(src_rows, (1 + negatives, 1))
    labels = (jnp.arange(pairs_dev, dtype=jnp.int32) < pos_rows).astype(jnp.float32)
    joint_rows = (left_rows.astype(jnp.float32) * right_rows.astype(jnp.float32)).astype(LOW)
    a_one = dot_plain(joint_rows, w_one) + b_one
    h_one = jax.nn.silu(a_one).astype(LOW)
    a_two = dot_plain(h_one, w_two) + b_two
    h_two = jax.nn.silu(a_two)
    scores = jnp.sum(h_two * w_out, axis=1)
    loss_slope = jax.nn.sigmoid(scores) - labels
    d_two = loss_slope[:, None] * w_out * silu_slope(a_two)
    d_two_low = d_two.astype(LOW)
    d_one = dot_last(d_two_low, w_two) * silu_slope(a_one)
    d_one_low = d_one.astype(LOW)
    d_joint = dot_last(d_one_low, w_one)
    scorer_term = (
        jnp.concatenate([dot_first(joint_rows, d_one_low), dot_first(h_one, d_two_low)], axis=0)
        / pairs_dev
    ).astype(LOW)
    d_left = d_joint * right_rows
    d_right = d_joint * left_rows
    grad_src = jnp.sum(d_left.reshape(1 + negatives, pos_rows, width), axis=0)
    grad_dst = d_right[:pos_rows] + dot_plain(
        pick_across(neg_flat, pos_rows), d_right[pos_rows:].astype(LOW)
    )
    end_grads = jnp.concatenate([grad_src, grad_dst], axis=0).astype(LOW)
    outbound = dot_plain(pick_across(ends, slots), end_grads).astype(LOW)
    received, scorer_share = return_rows(
        groups, inners, outbound.reshape(owners, padded, width), scorer_term
    )
    node_grads = dot_plain(pick_across(flat_lists, nodes), received.reshape(slots, width))
    d_pre = node_grads * silu_slope(pre_act)
    d_pre_low = d_pre.astype(LOW)
    grad_self = dot_last(d_pre_low, w_self).astype(LOW)
    grad_agg = dot_last(d_pre_low, w_nbr).astype(LOW)
    layer_term = (
        jnp.concatenate([dot_first(x_self, d_pre_low), dot_first(x_agg, d_pre_low)], axis=0)
        / pairs_dev
    ).astype(LOW)
    bias_term = (
        jnp.concatenate(
            [
                jnp.sum(d_one, axis=0),
                jnp.sum(d_two, axis=0),
                jnp.sum(loss_slope[:, None] * h_two, axis=0),
                jnp.sum(d_pre, axis=0),
            ]
        )
        / pairs_dev
    )
    layer_share, bias_total = share_layer(groups, inners, layer_term, bias_term)
    return (grad_self, grad_agg, scorer_share.reshape(-1), layer_share, bias_total)


def solution(mesh):
    rows = P(("group", "inner"), None)
    flat = P(("group", "inner"))
    return jax.shard_map(
        body,
        mesh=mesh,
        in_specs=(rows, rows) + (P(),) * 8 + (P(("group", "inner"), None, None), rows, rows),
        out_specs=(rows, rows, flat, flat, P()),
        check_vma=False,
    )
```

```python
import functools

import jax
import jax.numpy as jnp
from jax import lax
from jax.experimental import pallas as pl
from jax.experimental.pallas import tpu as pltpu
from jax.sharding import PartitionSpec as P

MESH = pl.DeviceIdType.MESH
VMEM = pltpu.VMEM
LOW = jnp.bfloat16


def silu_slope(inputs):
    sigmoid_of = jax.nn.sigmoid(inputs)
    return sigmoid_of * (1.0 + inputs * (1.0 - sigmoid_of))


def dot_first(first_op, second_op):
    return lax.dot_general(
        first_op, second_op, (((0,), (0,)), ((), ())), preferred_element_type=jnp.float32
    )


def dot_last(first_op, second_op):
    return lax.dot_general(
        first_op, second_op, (((1,), (1,)), ((), ())), preferred_element_type=jnp.float32
    )


def dot_plain(first_op, second_op):
    return jnp.dot(first_op, second_op, preferred_element_type=jnp.float32)


def place(groups, inners):
    group = lax.axis_index("group")
    inner = lax.axis_index("inner")
    return group, inner, group * inners + inner


def peer_of(groups, inners, step):
    _, _, me = place(groups, inners)
    return lax.rem(me + step, groups * inners)


def greet_all(groups, inners):
    barrier = pltpu.get_barrier_semaphore()

    def greet(step, carry):
        peer = peer_of(groups, inners, step)
        pl.semaphore_signal(
            barrier,
            inc=1,
            device_id=(peer // inners, lax.rem(peer, inners)),
            device_id_type=MESH,
        )
        return carry

    lax.fori_loop(1, groups * inners, greet, 0)


def exchange_copy(groups, inners, step, landing, src, dst, sends, recvs):
    _, _, me = place(groups, inners)
    peer = peer_of(groups, inners, step)
    slot = peer if landing else me
    return pltpu.make_async_remote_copy(
        src_ref=src.at[peer],
        dst_ref=dst.at[slot],
        send_sem=sends.at[peer],
        recv_sem=recvs.at[slot],
        device_id=(peer // inners, lax.rem(peer, inners)),
        device_id_type=MESH,
    )


def exchange(groups, inners, make, src, dst, sends, recvs):
    def start(step, carry):
        peer = peer_of(groups, inners, step)
        src[peer] = make(peer)
        exchange_copy(groups, inners, step, False, src, dst, sends, recvs).start()
        return carry

    lax.fori_loop(1, groups * inners, start, 0)
    _, _, me = place(groups, inners)
    dst[me] = make(me)


def exchange_wait(groups, inners, src, dst, sends, recvs):
    def finish(step, carry):
        copy = exchange_copy(groups, inners, step, True, src, dst, sends, recvs)
        copy.wait_send()
        copy.wait_recv()
        return carry

    lax.fori_loop(1, groups * inners, finish, 0)


def axis_copy(groups, inners, along, step, landing, src, dst, sends, recvs, whole):
    group, inner, _ = place(groups, inners)
    if along == "group":
        mine, peer = group, lax.rem(group + step, groups)
        device = (peer, inner)
    else:
        mine, peer = inner, lax.rem(inner + step, inners)
        device = (group, peer)
    slot = peer if landing else mine
    return pltpu.make_async_remote_copy(
        src_ref=src if whole else src.at[peer],
        dst_ref=dst.at[slot],
        send_sem=sends.at[peer],
        recv_sem=recvs.at[slot],
        device_id=device,
        device_id_type=MESH,
    )


def axis_start(groups, inners, along, src, dst, sends, recvs, whole=False):
    for step in range(1, groups if along == "group" else inners):
        axis_copy(
            groups, inners, along, step, False, src, dst, sends, recvs, whole
        ).start()


def axis_wait(groups, inners, along, src, dst, sends, recvs, whole=False):
    for step in range(1, groups if along == "group" else inners):
        copy = axis_copy(groups, inners, along, step, True, src, dst, sends, recvs, whole)
        copy.wait_send()
        copy.wait_recv()


def share_middle(groups, inners, halves, src, land_one, stage, land_two):
    group, inner, _ = place(groups, inners)
    land_one[group] = src[group]
    total = land_one[0].astype(jnp.float32)
    for index in range(1, groups):
        total = total + land_one[index].astype(jnp.float32)
    rows, width = total.shape[0] // inners, total.shape[1]
    half = width // halves
    for index in range(inners):
        part = total[index * rows : (index + 1) * rows]
        if halves > 1:
            part = jnp.concatenate(
                [part[:, side * half : (side + 1) * half] for side in range(halves)], axis=0
            )
        stage[index, : rows * halves] = part.astype(stage.dtype)
    land_two[inner] = stage[inner]


def sum_slots(count, landed):
    total = landed[0].astype(jnp.float32)
    for index in range(1, count):
        total = total + landed[index].astype(jnp.float32)
    return total


def hot(mask):
    return jnp.where(mask, 1.0, 0.0).astype(LOW)


def iota(rows, columns, dim):
    return lax.broadcasted_iota(jnp.int32, (rows, columns), dim)


def sigmoid(values):
    return 0.5 * jnp.tanh(0.5 * values) + 0.5


def kernel(
    groups,
    inners,
    block,
    x_self,
    x_agg,
    w_self,
    w_nbr,
    b_layer,
    w_one,
    b_one,
    w_two,
    b_two,
    w_out,
    lists_col,
    lists_row,
    ends_col,
    ends_row,
    neg_col,
    neg_row,
    grad_self,
    grad_agg,
    scorer_share,
    layer_share,
    bias_out,
    pre_act,
    table,
    outgoing,
    fetched,
    outbound,
    received,
    end_rows,
    end_grads,
    end_low,
    joint,
    h_one,
    d_two_low,
    d_one_low,
    weight_sum,
    hidden_sums,
    d_pre_low,
    layer_sum,
    terms_a,
    land_a,
    stage_a,
    final_a,
    terms_b,
    land_b,
    stage_b,
    final_b,
    bias,
    bias_land,
    bias_stage,
    bias_final,
    f_sends,
    f_recvs,
    r_sends,
    r_recvs,
    ag_sends,
    ag_recvs,
    ai_sends,
    ai_recvs,
    bg_sends,
    bg_recvs,
    bi_sends,
    bi_recvs,
    cg_sends,
    cg_recvs,
    ci_sends,
    ci_recvs,
):
    owners = groups * inners
    group, inner, me = place(groups, inners)
    nodes, width = x_self.shape
    padded = outgoing.shape[1]
    slots = owners * padded
    ends = end_rows.shape[0]
    pos = ends // 2
    halves = pos // block
    blocks = joint.shape[0]
    pairs = blocks * block
    hidden = w_two.shape[0]

    greet_all(groups, inners)

    def node_step(step, carry):
        rows = pl.ds(pl.multiple_of(step * block, block), block)
        acts = dot_plain(x_self[rows], w_self[...]) + dot_plain(x_agg[rows], w_nbr[...])
        acts = acts + b_layer[...]
        pre_act[rows] = acts
        table[rows] = (acts * sigmoid(acts)).astype(LOW)
        return carry

    lax.fori_loop(0, nodes // block, node_step, 0)
    pl.semaphore_wait(pltpu.get_barrier_semaphore(), owners - 1)

    def make_rows(peer):
        chosen = hot(lists_col[peer] == iota(padded, nodes, 1))
        return dot_plain(chosen, table[...]).astype(LOW)

    exchange(groups, inners, make_rows, outgoing, fetched, f_sends, f_recvs)
    exchange_wait(groups, inners, outgoing, fetched, f_sends, f_recvs)

    def end_step(step, carry):
        rows = pl.ds(pl.multiple_of(step * block, block), block)
        chosen = hot(ends_col[rows] == iota(block, slots, 1))
        all_rows = fetched[...].reshape(slots, width)
        end_rows[rows] = dot_plain(chosen, all_rows).astype(LOW)
        return carry

    lax.fori_loop(0, ends // block, end_step, 0)
    end_grads[...] = jnp.zeros_like(end_grads)
    hidden_sums[...] = jnp.zeros_like(hidden_sums)

    def pair_step(step, first):
        part = step if first else lax.rem(step, halves)
        rows = pl.ds(pl.multiple_of(part * block, block), block)
        dst_rows = pl.ds(pl.multiple_of(pos + part * block, block), block)
        left = end_rows[rows]
        if first:
            right = end_rows[dst_rows]
        else:
            chosen = hot(neg_col[step] == iota(block, pos, 1))
            right = dot_plain(chosen, end_rows[pos:]).astype(LOW)
        left = left.astype(jnp.float32)
        right = right.astype(jnp.float32)
        product = (left * right).astype(LOW)
        joint[step] = product
        a_one = dot_plain(product, w_one[...]) + b_one[...]
        s_one = sigmoid(a_one)
        slope_one = s_one * (1.0 + a_one * (1.0 - s_one))
        low_h = (a_one * s_one).astype(LOW)
        h_one[step] = low_h
        a_two = dot_plain(low_h, w_two[...]) + b_two[...]
        s_two = sigmoid(a_two)
        h_two = a_two * s_two
        scores = jnp.sum(h_two * w_out[...], axis=1, keepdims=True)
        slope = sigmoid(scores) - (1.0 if first else 0.0)
        d_two = slope * w_out[...] * (s_two * (1.0 + a_two * (1.0 - s_two)))
        low_two = d_two.astype(LOW)
        d_two_low[step] = low_two
        d_one = dot_last(low_two, w_two[...]) * slope_one
        low_one = d_one.astype(LOW)
        d_one_low[step] = low_one
        hidden_sums[0:1] += jnp.sum(d_one, axis=0, keepdims=True)
        hidden_sums[1:2] += jnp.sum(d_two, axis=0, keepdims=True)
        hidden_sums[2:3] += jnp.sum(slope * h_two, axis=0, keepdims=True)
        d_joint = dot_last(low_one, w_one[...])
        end_grads[rows] += d_joint * right
        d_right = d_joint * left
        if first:
            end_grads[dst_rows] += d_right
        else:
            back = hot(iota(pos, block, 0) == neg_row[step])
            end_grads[pos:] += dot_plain(back, d_right.astype(LOW))

    for step in range(halves):
        pair_step(step, True)

    def negative_step(step, carry):
        pair_step(step, False)
        return carry

    lax.fori_loop(halves, blocks, negative_step, 0)
    end_low[...] = end_grads[...].astype(LOW)

    def make_grads(peer):
        chosen = hot(iota(padded, ends, 0) + peer * padded == ends_row[...])
        return dot_plain(chosen, end_low[...]).astype(LOW)

    exchange(groups, inners, make_grads, outbound, received, r_sends, r_recvs)

    weight_sum[...] = jnp.zeros_like(weight_sum)

    def weight_step(step, carry):
        weight_sum[:width] += dot_first(joint[step], d_one_low[step])
        weight_sum[width:] += dot_first(h_one[step], d_two_low[step])
        return carry

    lax.fori_loop(0, blocks, weight_step, 0)
    chunk = weight_sum.shape[0] // groups
    for index in range(groups):
        part = weight_sum[index * chunk : (index + 1) * chunk]
        terms_a[index] = (part / pairs).astype(LOW)
    axis_start(groups, inners, "group", terms_a, land_a, ag_sends, ag_recvs)
    axis_wait(groups, inners, "group", terms_a, land_a, ag_sends, ag_recvs)
    share_middle(groups, inners, 2, terms_a, land_a, stage_a, final_a)
    axis_start(groups, inners, "inner", stage_a, final_a, ai_sends, ai_recvs)
    exchange_wait(groups, inners, outbound, received, r_sends, r_recvs)

    layer_sum[...] = jnp.zeros_like(layer_sum)
    hidden_sums[3:4] = jnp.zeros((1, hidden), jnp.float32)

    def layer_step(step, carry):
        rows = pl.ds(pl.multiple_of(step * block, block), block)
        chosen = hot(iota(block, slots, 0) + step * block == lists_row[...])
        sums = dot_plain(chosen, received[...].reshape(slots, width))
        acts = pre_act[rows]
        s_act = sigmoid(acts)
        d_pre = sums * (s_act * (1.0 + acts * (1.0 - s_act)))
        low = d_pre.astype(LOW)
        d_pre_low[rows] = low
        hidden_sums[3:4, :width] += jnp.sum(d_pre, axis=0, keepdims=True)
        layer_sum[:width] += dot_first(x_self[rows], low)
        layer_sum[width:] += dot_first(x_agg[rows], low)
        return carry

    lax.fori_loop(0, nodes // block, layer_step, 0)
    layer_chunk = layer_sum.shape[0] // groups
    for index in range(groups):
        part = layer_sum[index * layer_chunk : (index + 1) * layer_chunk]
        terms_b[index] = (part / pairs).astype(LOW)
    bias[...] = jnp.zeros_like(bias)
    line = 0
    for row, span in ((0, hidden), (1, hidden), (2, hidden), (3, width)):
        for piece in range(span // 128):
            values = hidden_sums[row : row + 1, piece * 128 : (piece + 1) * 128]
            bias[line : line + 1] = values / pairs
            line += 1
    axis_start(groups, inners, "group", terms_b, land_b, bg_sends, bg_recvs)
    axis_start(groups, inners, "group", bias, bias_land, cg_sends, cg_recvs, True)

    def out_step(step, carry):
        rows = pl.ds(pl.multiple_of(step * block, block), block)
        grad_self[rows] = dot_last(d_pre_low[rows], w_self[...]).astype(LOW)
        grad_agg[rows] = dot_last(d_pre_low[rows], w_nbr[...]).astype(LOW)
        return carry

    lax.fori_loop(0, nodes // block, out_step, 0)
    axis_wait(groups, inners, "group", terms_b, land_b, bg_sends, bg_recvs)
    share_middle(groups, inners, 1, terms_b, land_b, stage_b, final_b)
    axis_start(groups, inners, "inner", stage_b, final_b, bi_sends, bi_recvs)
    axis_wait(groups, inners, "group", bias, bias_land, cg_sends, cg_recvs, True)
    bias_land[group] = bias[...]
    bias_stage[...] = sum_slots(groups, bias_land)
    bias_final[inner] = bias_stage[...]
    axis_start(groups, inners, "inner", bias_stage, bias_final, ci_sends, ci_recvs, True)
    axis_wait(groups, inners, "inner", stage_a, final_a, ai_sends, ai_recvs)
    total = sum_slots(inners, final_a)
    rows = chunk // inners
    half = hidden // 2
    scorer_share[:, :half] = total[:rows]
    scorer_share[:, half:] = total[rows : 2 * rows]
    axis_wait(groups, inners, "inner", stage_b, final_b, bi_sends, bi_recvs)
    layer_share[...] = sum_slots(inners, final_b)[: layer_chunk // inners]
    axis_wait(groups, inners, "inner", bias_stage, bias_final, ci_sends, ci_recvs, True)
    bias_out[...] = sum_slots(inners, bias_final)


def up_to(count, step):
    return -(-count // step) * step


def body(
    x_self,
    x_agg,
    w_self,
    w_nbr,
    b_layer,
    w_one,
    b_one,
    w_two,
    b_two,
    w_out,
    send_lists,
    endpoint_slots,
    neg_index,
):
    groups = lax.axis_size("group")
    inners = lax.axis_size("inner")
    owners = groups * inners
    nodes, width = x_self.shape
    hidden = w_two.shape[0]
    pos = endpoint_slots.shape[0]
    negatives = neg_index.shape[1]
    capacity = send_lists.shape[2]
    padded = up_to(capacity, 16)
    slots = owners * padded
    block = 256
    blocks = pos * (1 + negatives) // block
    lists = send_lists.reshape(owners, capacity)
    ends = endpoint_slots.T.reshape(-1)
    if padded != capacity:
        lists = jnp.pad(lists, ((0, 0), (0, padded - capacity)), constant_values=-1)
        ends = ends + (ends // capacity) * (padded - capacity)
    own = jnp.arange(pos, dtype=jnp.int32)
    negs = jnp.concatenate([own, neg_index.T.reshape(-1)]).reshape(blocks, block)

    def f32(*shape):
        return VMEM(shape, jnp.float32)

    def low(*shape):
        return VMEM(shape, LOW)

    chunk_a = (width + hidden) // groups
    chunk_b = 2 * width // groups
    slab_a = up_to(2 * chunk_a // inners, 16)
    slab_b = up_to(chunk_b // inners, 16)
    lines = up_to((3 * hidden + width) // 128, 8)
    scratch = [
        f32(nodes, width),
        low(nodes, width),
        low(owners, padded, width),
        low(owners, padded, width),
        low(owners, padded, width),
        low(owners, padded, width),
        low(2 * pos, width),
        f32(2 * pos, width),
        low(2 * pos, width),
        low(blocks, block, width),
        low(blocks, block, hidden),
        low(blocks, block, hidden),
        low(blocks, block, hidden),
        f32(width + hidden, hidden),
        f32(8, hidden),
        low(nodes, width),
        f32(2 * width, width),
        low(groups, chunk_a, hidden),
        low(groups, chunk_a, hidden),
        low(inners, slab_a, hidden // 2),
        low(inners, slab_a, hidden // 2),
        low(groups, chunk_b, width),
        low(groups, chunk_b, width),
        low(inners, slab_b, width),
        low(inners, slab_b, width),
        f32(lines, 128),
        f32(groups, lines, 128),
        f32(lines, 128),
        f32(inners, lines, 128),
    ]
    counts = [owners] * 4 + ([groups] * 2 + [inners] * 2) * 3
    flops = 2 * (pos * (1 + negatives) * 3 * hidden * (width + hidden))
    grad_self, grad_agg, scorer_share, layer_share, total = pl.pallas_call(
        functools.partial(kernel, groups, inners, block),
        out_shape=(
            jax.ShapeDtypeStruct((nodes, width), LOW),
            jax.ShapeDtypeStruct((nodes, width), LOW),
            jax.ShapeDtypeStruct((chunk_a // inners, hidden), jnp.float32),
            jax.ShapeDtypeStruct((chunk_b // inners, width), jnp.float32),
            jax.ShapeDtypeStruct((lines, 128), jnp.float32),
        ),
        in_specs=[pl.BlockSpec(memory_space=VMEM)] * 16,
        out_specs=(pl.BlockSpec(memory_space=VMEM),) * 5,
        scratch_shapes=scratch + [pltpu.SemaphoreType.DMA((count,)) for count in counts],
        compiler_params=pltpu.CompilerParams(
            collective_id=0, has_side_effects=True, vmem_limit_bytes=56 * 1024 * 1024
        ),
        cost_estimate=pl.CostEstimate(flops=flops, bytes_accessed=2**23, transcendentals=2**22),
        name="link_backward",
    )(
        x_self,
        x_agg,
        w_self,
        w_nbr,
        b_layer[None],
        w_one,
        b_one[None],
        w_two,
        b_two[None],
        w_out[None],
        lists[:, :, None],
        lists.reshape(1, slots),
        ends[:, None],
        ends[None],
        negs[:, :, None],
        negs[:, None, :],
    )
    bias_total = total.reshape(-1)[: 3 * hidden + width]
    return (grad_self, grad_agg, scorer_share.reshape(-1), layer_share.reshape(-1), bias_total)


def solution(mesh):
    rows = P(("group", "inner"), None)
    flat = P(("group", "inner"))
    return jax.shard_map(
        body,
        mesh=mesh,
        in_specs=(rows, rows) + (P(),) * 8 + (P(("group", "inner"), None, None), rows, rows),
        out_specs=(rows, rows, flat, flat, P()),
        check_vma=False,
    )
```

```python
import functools

import jax
import jax.numpy as jnp
from jax import lax
from jax.experimental import pallas as pl
from jax.experimental.pallas import tpu as pltpu
from jax.sharding import PartitionSpec as P

MESH = pl.DeviceIdType.MESH
VMEM = pltpu.VMEM
LOW = jnp.bfloat16


def silu_slope(inputs):
    sigmoid_of = jax.nn.sigmoid(inputs)
    return sigmoid_of * (1.0 + inputs * (1.0 - sigmoid_of))


def dot_first(first_op, second_op):
    return lax.dot_general(
        first_op, second_op, (((0,), (0,)), ((), ())), preferred_element_type=jnp.float32
    )


def dot_last(first_op, second_op):
    return lax.dot_general(
        first_op, second_op, (((1,), (1,)), ((), ())), preferred_element_type=jnp.float32
    )


def dot_plain(first_op, second_op):
    return jnp.dot(first_op, second_op, preferred_element_type=jnp.float32)


def place(groups, inners):
    group = lax.axis_index("group")
    inner = lax.axis_index("inner")
    return group, inner, group * inners + inner


def peer_of(groups, inners, step):
    group, inner, _ = place(groups, inners)
    middle = inners // 2
    turn = step - 1
    turn = turn + jnp.where(turn >= (inners - middle) * groups, 1, 0)
    to_inner = lax.rem(inner + middle + turn // groups, inners)
    return lax.rem(group + lax.rem(turn, groups), groups) * inners + to_inner


def greet_all(groups, inners):
    barrier = pltpu.get_barrier_semaphore()

    def greet(step, carry):
        peer = peer_of(groups, inners, step)
        pl.semaphore_signal(
            barrier,
            inc=1,
            device_id=(peer // inners, lax.rem(peer, inners)),
            device_id_type=MESH,
        )
        return carry

    lax.fori_loop(1, groups * inners, greet, 0)


def exchange_copy(groups, inners, step, landing, src, dst, sends, recvs):
    _, _, me = place(groups, inners)
    peer = peer_of(groups, inners, step)
    slot = peer if landing else me
    return pltpu.make_async_remote_copy(
        src_ref=src.at[peer],
        dst_ref=dst.at[slot],
        send_sem=sends.at[peer],
        recv_sem=recvs.at[slot],
        device_id=(peer // inners, lax.rem(peer, inners)),
        device_id_type=MESH,
    )


def exchange(groups, inners, make, src, dst, sends, recvs):
    def start(step, carry):
        peer = peer_of(groups, inners, step)
        src[peer] = make(peer)
        exchange_copy(groups, inners, step, False, src, dst, sends, recvs).start()
        return carry

    lax.fori_loop(1, groups * inners, start, 0)
    _, _, me = place(groups, inners)
    dst[me] = make(me)


def exchange_wait(groups, inners, src, dst, sends, recvs):
    def finish(step, carry):
        copy = exchange_copy(groups, inners, step, True, src, dst, sends, recvs)
        copy.wait_send()
        copy.wait_recv()
        return carry

    lax.fori_loop(1, groups * inners, finish, 0)


def axis_copy(groups, inners, along, step, landing, src, dst, sends, recvs, whole):
    group, inner, _ = place(groups, inners)
    if along == "group":
        mine, peer = group, lax.rem(group + step, groups)
        device = (peer, inner)
    else:
        mine, peer = inner, lax.rem(inner + step, inners)
        device = (group, peer)
    slot = peer if landing else mine
    return pltpu.make_async_remote_copy(
        src_ref=src if whole else src.at[peer],
        dst_ref=dst.at[slot],
        send_sem=sends.at[peer],
        recv_sem=recvs.at[slot],
        device_id=device,
        device_id_type=MESH,
    )


def axis_start(groups, inners, along, src, dst, sends, recvs, whole=False):
    for step in range(1, groups if along == "group" else inners):
        axis_copy(
            groups, inners, along, step, False, src, dst, sends, recvs, whole
        ).start()


def axis_wait(groups, inners, along, src, dst, sends, recvs, whole=False):
    for step in range(1, groups if along == "group" else inners):
        copy = axis_copy(groups, inners, along, step, True, src, dst, sends, recvs, whole)
        copy.wait_send()
        copy.wait_recv()


def share_middle(groups, inners, halves, src, land_one, stage, land_two):
    group, inner, _ = place(groups, inners)
    land_one[group] = src[group]
    total = land_one[0].astype(jnp.float32)
    for index in range(1, groups):
        total = total + land_one[index].astype(jnp.float32)
    rows, width = total.shape[0] // inners, total.shape[1]
    half = width // halves
    for index in range(inners):
        part = total[index * rows : (index + 1) * rows]
        if halves > 1:
            part = jnp.concatenate(
                [part[:, side * half : (side + 1) * half] for side in range(halves)], axis=0
            )
        stage[index, : rows * halves] = part.astype(stage.dtype)
    land_two[inner] = stage[inner]


def sum_slots(count, landed):
    total = landed[0].astype(jnp.float32)
    for index in range(1, count):
        total = total + landed[index].astype(jnp.float32)
    return total


def hot(mask):
    return jnp.where(mask, 1.0, 0.0).astype(LOW)


def iota(rows, columns, dim):
    return lax.broadcasted_iota(jnp.int32, (rows, columns), dim)


def sigmoid(values):
    return 0.5 * jnp.tanh(0.5 * values) + 0.5


def kernel(
    groups,
    inners,
    block,
    x_self,
    x_agg,
    w_self,
    w_nbr,
    b_layer,
    w_one,
    b_one,
    w_two,
    b_two,
    w_out,
    lists,
    ends_pair,
    negs,
    d_pre_low,
    scorer_share,
    layer_share,
    bias_out,
    pre_act,
    table,
    outgoing,
    fetched,
    outbound,
    received,
    end_rows,
    end_grads,
    end_low,
    joint,
    h_one,
    d_two_low,
    d_one_low,
    weight_sum,
    hidden_sums,
    layer_sum,
    terms_a,
    land_a,
    stage_a,
    final_a,
    terms_b,
    land_b,
    stage_b,
    final_b,
    bias,
    bias_land,
    bias_stage,
    bias_final,
    lists_wide,
    lists_tall,
    lists_row,
    index_wide,
    index_tall,
    ends_row,
    f_sends,
    f_recvs,
    r_sends,
    r_recvs,
    ag_sends,
    ag_recvs,
    ai_sends,
    ai_recvs,
    bg_sends,
    bg_recvs,
    bi_sends,
    bi_recvs,
    cg_sends,
    cg_recvs,
    ci_sends,
    ci_recvs,
):
    owners = groups * inners
    group, inner, me = place(groups, inners)
    nodes, width = x_self.shape
    padded = outgoing.shape[1]
    slots = owners * padded
    ends = end_rows.shape[0]
    pos = ends // 2
    halves = pos // block
    blocks = joint.shape[0]
    pairs = blocks * block
    hidden = w_two.shape[0]

    greet_all(groups, inners)
    lists_wide[...] = jnp.zeros_like(lists_wide)
    lists_wide[:owners, :padded] = lists[...].astype(jnp.float32)
    lists_tall[...] = jnp.transpose(lists_wide[...])

    def column(values, index):
        chosen = jnp.where(iota(*values.shape, 1) == index, values, 0.0)
        return jnp.sum(chosen, axis=1, keepdims=True).astype(jnp.int32)

    def node_step(step, carry):
        rows = pl.ds(pl.multiple_of(step * block, block), block)
        acts = dot_plain(x_self[rows], w_self[...]) + dot_plain(x_agg[rows], w_nbr[...])
        acts = acts + b_layer[...]
        pre_act[rows] = acts
        table[rows] = (acts * sigmoid(acts)).astype(LOW)
        return carry

    lax.fori_loop(0, nodes // block, node_step, 0)
    pl.semaphore_wait(pltpu.get_barrier_semaphore(), owners - 1)

    def make_rows(peer):
        chosen = hot(column(lists_tall[:padded], peer) == iota(padded, nodes, 1))
        return dot_plain(chosen, table[...]).astype(LOW)

    exchange(groups, inners, make_rows, outgoing, fetched, f_sends, f_recvs)


    index_wide[...] = jnp.zeros_like(index_wide)
    index_wide[:2] = ends_pair[...].astype(jnp.float32)
    index_wide[2 : 2 + negs.shape[0]] = negs[...].astype(jnp.float32)
    index_tall[...] = jnp.transpose(index_wide[...])
    for side in range(2):
        ends_row[:, side * pos : (side + 1) * pos] = ends_pair[side : side + 1]
    for owner in range(owners):
        lists_row[:, owner * padded : (owner + 1) * padded] = lists[owner : owner + 1]
    end_grads[...] = jnp.zeros_like(end_grads)
    hidden_sums[...] = jnp.zeros_like(hidden_sums)
    weight_sum[...] = jnp.zeros_like(weight_sum)
    exchange_wait(groups, inners, outgoing, fetched, f_sends, f_recvs)

    def end_step(step, carry):
        rows = pl.ds(pl.multiple_of(step * block, block), block)
        part = pl.ds(pl.multiple_of(lax.rem(step, halves) * block, block), block)
        chosen = hot(column(index_tall[part], step // halves) == iota(block, slots, 1))
        all_rows = fetched[...].reshape(slots, width)
        end_rows[rows] = dot_plain(chosen, all_rows).astype(LOW)
        return carry

    lax.fori_loop(0, ends // block, end_step, 0)

    def pair_step(step, first):
        part = step if first else lax.rem(step, halves)
        rows = pl.ds(pl.multiple_of(part * block, block), block)
        dst_rows = pl.ds(pl.multiple_of(pos + part * block, block), block)
        left = end_rows[rows]
        if first:
            right = end_rows[dst_rows]
        else:
            chosen = hot(column(index_tall[rows], 1 + step // halves) == iota(block, pos, 1))
            right = dot_plain(chosen, end_rows[pos:]).astype(LOW)
        left = left.astype(jnp.float32)
        right = right.astype(jnp.float32)
        product = (left * right).astype(LOW)
        joint[step] = product
        a_one = dot_plain(product, w_one[...]) + b_one[...]
        s_one = sigmoid(a_one)
        slope_one = s_one * (1.0 + a_one * (1.0 - s_one))
        low_h = (a_one * s_one).astype(LOW)
        h_one[step] = low_h
        a_two = dot_plain(low_h, w_two[...]) + b_two[...]
        s_two = sigmoid(a_two)
        h_two = a_two * s_two
        scores = jnp.sum(h_two * w_out[...], axis=1, keepdims=True)
        slope = sigmoid(scores) - (1.0 if first else 0.0)
        d_two = slope * w_out[...] * (s_two * (1.0 + a_two * (1.0 - s_two)))
        low_two = d_two.astype(LOW)
        d_two_low[step] = low_two
        d_one = dot_last(low_two, w_two[...]) * slope_one
        low_one = d_one.astype(LOW)
        d_one_low[step] = low_one
        hidden_sums[0:1] += jnp.sum(d_one, axis=0, keepdims=True)
        hidden_sums[1:2] += jnp.sum(d_two, axis=0, keepdims=True)
        hidden_sums[2:3] += jnp.sum(slope * h_two, axis=0, keepdims=True)
        d_joint = dot_last(low_one, w_one[...])
        end_grads[rows] += d_joint * right
        d_right = d_joint * left
        if first:
            end_grads[dst_rows] += d_right
        else:
            along = negs[pl.ds(step // halves - 1, 1), rows]
            back = hot(iota(pos, block, 0) == along)
            end_grads[pos:] += dot_plain(back, d_right.astype(LOW))

    for step in range(halves):
        pair_step(step, True)

    def negative_step(step, carry):
        pair_step(step, False)
        return carry

    lax.fori_loop(halves, blocks, negative_step, 0)
    end_low[...] = end_grads[...].astype(LOW)

    def make_grads(peer):
        chosen = hot(iota(padded, ends, 0) + peer * padded == ends_row[...])
        return dot_plain(chosen, end_low[...]).astype(LOW)

    exchange(groups, inners, make_grads, outbound, received, r_sends, r_recvs)

    def weight_step(step, carry):
        weight_sum[:width] += dot_first(joint[step], d_one_low[step])
        weight_sum[width:] += dot_first(h_one[step], d_two_low[step])
        return carry

    lax.fori_loop(0, blocks, weight_step, 0)
    chunk = weight_sum.shape[0] // groups
    for index in range(groups):
        part = weight_sum[index * chunk : (index + 1) * chunk]
        terms_a[index] = (part / pairs).astype(LOW)
    axis_start(groups, inners, "group", terms_a, land_a, ag_sends, ag_recvs)
    axis_wait(groups, inners, "group", terms_a, land_a, ag_sends, ag_recvs)
    share_middle(groups, inners, 2, terms_a, land_a, stage_a, final_a)
    axis_start(groups, inners, "inner", stage_a, final_a, ai_sends, ai_recvs)
    exchange_wait(groups, inners, outbound, received, r_sends, r_recvs)

    layer_sum[...] = jnp.zeros_like(layer_sum)
    hidden_sums[3:4] = jnp.zeros((1, hidden), jnp.float32)

    def layer_step(step, carry):
        rows = pl.ds(pl.multiple_of(step * block, block), block)
        chosen = hot(iota(block, slots, 0) + step * block == lists_row[...])
        sums = dot_plain(chosen, received[...].reshape(slots, width))
        acts = pre_act[rows]
        s_act = sigmoid(acts)
        d_pre = sums * (s_act * (1.0 + acts * (1.0 - s_act)))
        low = d_pre.astype(LOW)
        d_pre_low[rows] = low
        hidden_sums[3:4, :width] += jnp.sum(d_pre, axis=0, keepdims=True)
        layer_sum[:width] += dot_first(x_self[rows], low)
        layer_sum[width:] += dot_first(x_agg[rows], low)
        return carry

    lax.fori_loop(0, nodes // block, layer_step, 0)
    layer_chunk = layer_sum.shape[0] // groups
    for index in range(groups):
        part = layer_sum[index * layer_chunk : (index + 1) * layer_chunk]
        terms_b[index] = (part / pairs).astype(LOW)
    bias[...] = jnp.zeros_like(bias)
    line = 0
    for row, span in ((0, hidden), (1, hidden), (2, hidden), (3, width)):
        for piece in range(span // 128):
            values = hidden_sums[row : row + 1, piece * 128 : (piece + 1) * 128]
            bias[line : line + 1] = values / pairs
            line += 1
    axis_start(groups, inners, "group", terms_b, land_b, bg_sends, bg_recvs)
    axis_start(groups, inners, "group", bias, bias_land, cg_sends, cg_recvs, True)
    axis_wait(groups, inners, "group", terms_b, land_b, bg_sends, bg_recvs)
    share_middle(groups, inners, 1, terms_b, land_b, stage_b, final_b)
    axis_start(groups, inners, "inner", stage_b, final_b, bi_sends, bi_recvs)
    axis_wait(groups, inners, "group", bias, bias_land, cg_sends, cg_recvs, True)
    bias_land[group] = bias[...]
    bias_stage[...] = sum_slots(groups, bias_land)
    bias_final[inner] = bias_stage[...]
    axis_start(groups, inners, "inner", bias_stage, bias_final, ci_sends, ci_recvs, True)
    axis_wait(groups, inners, "inner", stage_a, final_a, ai_sends, ai_recvs)
    total = sum_slots(inners, final_a)
    rows = chunk // inners
    half = hidden // 2
    scorer_share[:, :half] = total[:rows]
    scorer_share[:, half:] = total[rows : 2 * rows]
    axis_wait(groups, inners, "inner", stage_b, final_b, bi_sends, bi_recvs)
    layer_share[...] = sum_slots(inners, final_b)[: layer_chunk // inners]
    axis_wait(groups, inners, "inner", bias_stage, bias_final, ci_sends, ci_recvs, True)
    bias_out[...] = sum_slots(inners, bias_final)


def end_kernel(
    d_pre_low,
    w_self,
    w_nbr,
    scorer_share,
    layer_share,
    bias,
    grad_self,
    grad_agg,
    scorer_flat,
    layer_flat,
    bias_flat,
):
    grad_self[...] = dot_last(d_pre_low[...], w_self[...]).astype(LOW)
    grad_agg[...] = dot_last(d_pre_low[...], w_nbr[...]).astype(LOW)
    for share, flat in ((scorer_share, scorer_flat), (layer_share, layer_flat)):
        rows, width = share.shape
        lines = width // 128
        for line in range(lines):
            flat[pl.ds(line, rows, stride=lines)] = share[:, line * 128 : (line + 1) * 128]
    for line in range(bias_flat.shape[0] // 128):
        bias_flat[line * 128 : (line + 1) * 128] = bias[line]


def up_to(count, step):
    return -(-count // step) * step


def body(
    x_self,
    x_agg,
    w_self,
    w_nbr,
    b_layer,
    w_one,
    b_one,
    w_two,
    b_two,
    w_out,
    send_lists,
    endpoint_slots,
    neg_index,
):
    groups = lax.axis_size("group")
    inners = lax.axis_size("inner")
    owners = groups * inners
    nodes, width = x_self.shape
    hidden = w_two.shape[0]
    pos = endpoint_slots.shape[0]
    negatives = neg_index.shape[1]
    capacity = send_lists.shape[2]
    padded = up_to(capacity, 16)
    slots = owners * padded
    block = min(512, pos)
    blocks = pos * (1 + negatives) // block
    lists = send_lists.reshape(owners, capacity)
    ends = endpoint_slots.T
    negs = neg_index.T
    if padded != capacity:
        lists = jnp.pad(lists, ((0, 0), (0, padded - capacity)), constant_values=-1)
        ends = ends + (ends // capacity) * (padded - capacity)

    def f32(*shape):
        return VMEM(shape, jnp.float32)

    def low(*shape):
        return VMEM(shape, LOW)

    chunk_a = (width + hidden) // groups
    chunk_b = 2 * width // groups
    slab_a = up_to(2 * chunk_a // inners, 16)
    slab_b = up_to(chunk_b // inners, 16)
    lines = up_to((3 * hidden + width) // 128, 8)
    scratch = [
        f32(nodes, width),
        low(nodes, width),
        low(owners, padded, width),
        low(owners, padded, width),
        low(owners, padded, width),
        low(owners, padded, width),
        low(2 * pos, width),
        f32(2 * pos, width),
        low(2 * pos, width),
        low(blocks, block, width),
        low(blocks, block, hidden),
        low(blocks, block, hidden),
        low(blocks, block, hidden),
        f32(width + hidden, hidden),
        f32(8, hidden),
        f32(2 * width, width),
        low(groups, chunk_a, hidden),
        low(groups, chunk_a, hidden),
        low(inners, slab_a, hidden // 2),
        low(inners, slab_a, hidden // 2),
        low(groups, chunk_b, width),
        low(groups, chunk_b, width),
        low(inners, slab_b, width),
        low(inners, slab_b, width),
        f32(lines, 128),
        f32(groups, lines, 128),
        f32(lines, 128),
        f32(inners, lines, 128),
        f32(up_to(owners, 128), up_to(padded, 128)),
        f32(up_to(padded, 128), up_to(owners, 128)),
        VMEM((1, slots), jnp.int32),
        f32(128, pos),
        f32(pos, 128),
        VMEM((1, 2 * pos), jnp.int32),
    ]
    counts = [owners] * 4 + ([groups] * 2 + [inners] * 2) * 3
    flops = 2 * (pos * (1 + negatives) * 3 * hidden * (width + hidden))
    d_pre_low, scorer_share, layer_share, total = pl.pallas_call(
        functools.partial(kernel, groups, inners, block),
        out_shape=(
            jax.ShapeDtypeStruct((nodes, width), LOW),
            jax.ShapeDtypeStruct((chunk_a // inners, hidden), jnp.float32),
            jax.ShapeDtypeStruct((chunk_b // inners, width), jnp.float32),
            jax.ShapeDtypeStruct((lines, 128), jnp.float32),
        ),
        in_specs=[pl.BlockSpec(memory_space=VMEM)] * 13,
        out_specs=(pl.BlockSpec(memory_space=VMEM),) * 4,
        scratch_shapes=scratch + [pltpu.SemaphoreType.DMA((count,)) for count in counts],
        compiler_params=pltpu.CompilerParams(
            collective_id=0, has_side_effects=True, vmem_limit_bytes=56 * 1024 * 1024
        ),
        cost_estimate=pl.CostEstimate(flops=flops, bytes_accessed=2**23, transcendentals=2**22),
        name="link_backward",
    )(
        x_self,
        x_agg,
        w_self,
        w_nbr,
        b_layer[None],
        w_one,
        b_one[None],
        w_two,
        b_two[None],
        w_out[None],
        lists,
        ends,
        negs,
    )
    share_a, share_b = scorer_share.size, layer_share.size
    grad_self, grad_agg, scorer_flat, layer_flat, bias_total = pl.pallas_call(
        end_kernel,
        out_shape=(
            jax.ShapeDtypeStruct((nodes, width), LOW),
            jax.ShapeDtypeStruct((nodes, width), LOW),
            jax.ShapeDtypeStruct((share_a // 128, 128), jnp.float32),
            jax.ShapeDtypeStruct((share_b // 128, 128), jnp.float32),
            jax.ShapeDtypeStruct((3 * hidden + width,), jnp.float32),
        ),
        in_specs=[pl.BlockSpec(memory_space=VMEM)] * 6,
        out_specs=(pl.BlockSpec(memory_space=VMEM),) * 5,
        compiler_params=pltpu.CompilerParams(vmem_limit_bytes=32 * 1024 * 1024),
        name="end_products",
    )(d_pre_low, w_self, w_nbr, scorer_share, layer_share, total)
    return (grad_self, grad_agg, scorer_flat.reshape(-1), layer_flat.reshape(-1), bias_total)


def solution(mesh):
    rows = P(("group", "inner"), None)
    flat = P(("group", "inner"))
    return jax.shard_map(
        body,
        mesh=mesh,
        in_specs=(rows, rows) + (P(),) * 8 + (P(("group", "inner"), None, None), rows, rows),
        out_specs=(rows, rows, flat, flat, P()),
        check_vma=False,
    )
```

```python
import functools

import jax
import jax.numpy as jnp
from jax import lax
from jax.experimental import pallas as pl
from jax.experimental.pallas import tpu as pltpu
from jax.sharding import PartitionSpec as P

MESH = pl.DeviceIdType.MESH
VMEM = pltpu.VMEM
LOW = jnp.bfloat16


def silu_slope(inputs):
    sigmoid_of = jax.nn.sigmoid(inputs)
    return sigmoid_of * (1.0 + inputs * (1.0 - sigmoid_of))


def dot_first(first_op, second_op):
    return lax.dot_general(
        first_op, second_op, (((0,), (0,)), ((), ())), preferred_element_type=jnp.float32
    )


def dot_last(first_op, second_op):
    return lax.dot_general(
        first_op, second_op, (((1,), (1,)), ((), ())), preferred_element_type=jnp.float32
    )


def dot_plain(first_op, second_op):
    return jnp.dot(first_op, second_op, preferred_element_type=jnp.float32)


def place(groups, inners):
    group = lax.axis_index("group")
    inner = lax.axis_index("inner")
    return group, inner, group * inners + inner


def peer_of(groups, inners, step):
    group, inner, _ = place(groups, inners)
    middle = inners // 2
    turn = step - 1
    turn = turn + jnp.where(turn >= (inners - middle) * groups, 1, 0)
    to_inner = lax.rem(inner + middle + turn // groups, inners)
    return lax.rem(group + lax.rem(turn, groups), groups) * inners + to_inner


def greet_all(groups, inners):
    barrier = pltpu.get_barrier_semaphore()

    def greet(step, carry):
        peer = peer_of(groups, inners, step)
        pl.semaphore_signal(
            barrier,
            inc=1,
            device_id=(peer // inners, lax.rem(peer, inners)),
            device_id_type=MESH,
        )
        return carry

    lax.fori_loop(1, groups * inners, greet, 0)


def exchange_copy(groups, inners, step, landing, src, dst, sends, recvs):
    _, _, me = place(groups, inners)
    peer = peer_of(groups, inners, step)
    slot = peer if landing else me
    return pltpu.make_async_remote_copy(
        src_ref=src.at[peer],
        dst_ref=dst.at[slot],
        send_sem=sends.at[peer],
        recv_sem=recvs.at[slot],
        device_id=(peer // inners, lax.rem(peer, inners)),
        device_id_type=MESH,
    )


def exchange(groups, inners, make, src, dst, sends, recvs):
    def start(step, carry):
        peer = peer_of(groups, inners, step)
        src[peer] = make(peer)
        exchange_copy(groups, inners, step, False, src, dst, sends, recvs).start()
        return carry

    lax.fori_loop(1, groups * inners, start, 0)
    _, _, me = place(groups, inners)
    dst[me] = make(me)


def exchange_wait(groups, inners, src, dst, sends, recvs):
    def finish(step, carry):
        copy = exchange_copy(groups, inners, step, True, src, dst, sends, recvs)
        copy.wait_send()
        copy.wait_recv()
        return carry

    lax.fori_loop(1, groups * inners, finish, 0)


def axis_copy(groups, inners, along, step, landing, src, dst, sends, recvs, whole):
    group, inner, _ = place(groups, inners)
    if along == "group":
        mine, peer = group, lax.rem(group + step, groups)
        device = (peer, inner)
    else:
        mine, peer = inner, lax.rem(inner + step, inners)
        device = (group, peer)
    slot = peer if landing else mine
    return pltpu.make_async_remote_copy(
        src_ref=src if whole else src.at[peer],
        dst_ref=dst.at[slot],
        send_sem=sends.at[peer],
        recv_sem=recvs.at[slot],
        device_id=device,
        device_id_type=MESH,
    )


def axis_start(groups, inners, along, src, dst, sends, recvs, whole=False):
    for step in range(1, groups if along == "group" else inners):
        axis_copy(
            groups, inners, along, step, False, src, dst, sends, recvs, whole
        ).start()


def axis_wait(groups, inners, along, src, dst, sends, recvs, whole=False):
    for step in range(1, groups if along == "group" else inners):
        copy = axis_copy(groups, inners, along, step, True, src, dst, sends, recvs, whole)
        copy.wait_send()
        copy.wait_recv()


def share_middle(groups, inners, halves, src, land_one, stage, land_two):
    group, inner, _ = place(groups, inners)
    land_one[group] = src[group]
    total = land_one[0].astype(jnp.float32)
    for index in range(1, groups):
        total = total + land_one[index].astype(jnp.float32)
    rows, width = total.shape[0] // inners, total.shape[1]
    half = width // halves
    for index in range(inners):
        part = total[index * rows : (index + 1) * rows]
        if halves > 1:
            part = jnp.concatenate(
                [part[:, side * half : (side + 1) * half] for side in range(halves)], axis=0
            )
        stage[index, : rows * halves] = part.astype(stage.dtype)
    land_two[inner] = stage[inner]


def sum_slots(count, landed):
    total = landed[0].astype(jnp.float32)
    for index in range(1, count):
        total = total + landed[index].astype(jnp.float32)
    return total


def hot(mask):
    return jnp.where(mask, 1.0, 0.0).astype(LOW)


def iota(rows, columns, dim):
    return lax.broadcasted_iota(jnp.int32, (rows, columns), dim)


def sigmoid(values):
    return 0.5 * jnp.tanh(0.5 * values) + 0.5


def kernel(
    groups,
    inners,
    block,
    x_self,
    x_agg,
    w_self,
    w_nbr,
    b_layer,
    w_one,
    b_one,
    w_two,
    b_two,
    w_out,
    lists,
    ends_pair,
    negs,
    d_pre_low,
    scorer_share,
    layer_share,
    bias_out,
    pre_act,
    table,
    outgoing,
    fetched,
    outbound,
    received,
    end_rows,
    end_grads,
    end_low,
    joint,
    h_one,
    d_two_low,
    d_one_low,
    weight_sum,
    hidden_sums,
    layer_sum,
    terms_a,
    land_a,
    stage_a,
    final_a,
    terms_b,
    land_b,
    stage_b,
    final_b,
    bias,
    bias_land,
    bias_stage,
    bias_final,
    lists_wide,
    lists_tall,
    lists_row,
    index_wide,
    index_tall,
    ends_row,
    f_sends,
    f_recvs,
    r_sends,
    r_recvs,
    ag_sends,
    ag_recvs,
    ai_sends,
    ai_recvs,
    bg_sends,
    bg_recvs,
    bi_sends,
    bi_recvs,
    cg_sends,
    cg_recvs,
    ci_sends,
    ci_recvs,
):
    owners = groups * inners
    group, inner, me = place(groups, inners)
    nodes, width = x_self.shape
    padded = outgoing.shape[1]
    slots = owners * padded
    ends = end_rows.shape[0]
    pos = ends // 2
    halves = pos // block
    blocks = joint.shape[0]
    pairs = blocks * block
    hidden = w_two.shape[0]

    greet_all(groups, inners)
    lists_wide[...] = jnp.zeros_like(lists_wide)
    lists_wide[:owners, :padded] = lists[...].astype(jnp.float32)
    lists_tall[...] = jnp.transpose(lists_wide[...])

    def column(values, index):
        chosen = jnp.where(iota(*values.shape, 1) == index, values, 0.0)
        return jnp.sum(chosen, axis=1, keepdims=True).astype(jnp.int32)

    def node_step(step, carry):
        rows = pl.ds(pl.multiple_of(step * block, block), block)
        acts = dot_plain(x_self[rows], w_self[...]) + dot_plain(x_agg[rows], w_nbr[...])
        acts = acts + b_layer[...]
        pre_act[rows] = acts
        table[rows] = (acts * sigmoid(acts)).astype(LOW)
        return carry

    lax.fori_loop(0, nodes // block, node_step, 0)
    pl.semaphore_wait(pltpu.get_barrier_semaphore(), owners - 1)

    def make_rows(peer):
        chosen = hot(column(lists_tall[:padded], peer) == iota(padded, nodes, 1))
        return dot_plain(chosen, table[...]).astype(LOW)

    exchange(groups, inners, make_rows, outgoing, fetched, f_sends, f_recvs)


    index_wide[...] = jnp.zeros_like(index_wide)
    index_wide[:2] = ends_pair[...].astype(jnp.float32)
    index_wide[2 : 2 + negs.shape[0]] = negs[...].astype(jnp.float32)
    index_tall[...] = jnp.transpose(index_wide[...])
    for side in range(2):
        ends_row[:, side * pos : (side + 1) * pos] = ends_pair[side : side + 1]
    for owner in range(owners):
        lists_row[:, owner * padded : (owner + 1) * padded] = lists[owner : owner + 1]
    end_grads[...] = jnp.zeros_like(end_grads)
    hidden_sums[...] = jnp.zeros_like(hidden_sums)
    weight_sum[...] = jnp.zeros_like(weight_sum)
    exchange_wait(groups, inners, outgoing, fetched, f_sends, f_recvs)

    def end_step(step, carry):
        rows = pl.ds(pl.multiple_of(step * block, block), block)
        part = pl.ds(pl.multiple_of(lax.rem(step, halves) * block, block), block)
        chosen = hot(column(index_tall[part], step // halves) == iota(block, slots, 1))
        all_rows = fetched[...].reshape(slots, width)
        end_rows[rows] = dot_plain(chosen, all_rows).astype(LOW)
        return carry

    lax.fori_loop(0, ends // block, end_step, 0)

    def pair_step(step, first):
        part = step if first else lax.rem(step, halves)
        rows = pl.ds(pl.multiple_of(part * block, block), block)
        dst_rows = pl.ds(pl.multiple_of(pos + part * block, block), block)
        left = end_rows[rows]
        if first:
            right = end_rows[dst_rows]
        else:
            chosen = hot(column(index_tall[rows], 1 + step // halves) == iota(block, pos, 1))
            right = dot_plain(chosen, end_rows[pos:]).astype(LOW)
        left = left.astype(jnp.float32)
        right = right.astype(jnp.float32)
        product = (left * right).astype(LOW)
        joint[step] = product
        a_one = dot_plain(product, w_one[...]) + b_one[...]
        s_one = sigmoid(a_one)
        slope_one = s_one * (1.0 + a_one * (1.0 - s_one))
        low_h = (a_one * s_one).astype(LOW)
        h_one[step] = low_h
        a_two = dot_plain(low_h, w_two[...]) + b_two[...]
        s_two = sigmoid(a_two)
        h_two = a_two * s_two
        scores = jnp.sum(h_two * w_out[...], axis=1, keepdims=True)
        slope = sigmoid(scores) - (1.0 if first else 0.0)
        d_two = slope * w_out[...] * (s_two * (1.0 + a_two * (1.0 - s_two)))
        low_two = d_two.astype(LOW)
        d_two_low[step] = low_two
        d_one = dot_last(low_two, w_two[...]) * slope_one
        low_one = d_one.astype(LOW)
        d_one_low[step] = low_one
        hidden_sums[0:1] += jnp.sum(d_one, axis=0, keepdims=True)
        hidden_sums[1:2] += jnp.sum(d_two, axis=0, keepdims=True)
        hidden_sums[2:3] += jnp.sum(slope * h_two, axis=0, keepdims=True)
        d_joint = dot_last(low_one, w_one[...])
        end_grads[rows] += d_joint * right
        d_right = d_joint * left
        if first:
            end_grads[dst_rows] += d_right
        else:
            along = negs[pl.ds(step // halves - 1, 1), rows]
            back = hot(iota(pos, block, 0) == along)
            end_grads[pos:] += dot_plain(back, d_right.astype(LOW))

    for step in range(halves):
        pair_step(step, True)

    def negative_step(step, carry):
        pair_step(step, False)
        return carry

    lax.fori_loop(halves, blocks, negative_step, 0)
    end_low[...] = end_grads[...].astype(LOW)

    def make_grads(peer):
        chosen = hot(iota(padded, ends, 0) + peer * padded == ends_row[...])
        return dot_plain(chosen, end_low[...]).astype(LOW)

    exchange(groups, inners, make_grads, outbound, received, r_sends, r_recvs)

    def weight_step(step, carry):
        weight_sum[:width] += dot_first(joint[step], d_one_low[step])
        weight_sum[width:] += dot_first(h_one[step], d_two_low[step])
        return carry

    lax.fori_loop(0, blocks, weight_step, 0)
    chunk = weight_sum.shape[0] // groups
    for index in range(groups):
        part = weight_sum[index * chunk : (index + 1) * chunk]
        terms_a[index] = (part / pairs).astype(LOW)
    axis_start(groups, inners, "group", terms_a, land_a, ag_sends, ag_recvs)
    axis_wait(groups, inners, "group", terms_a, land_a, ag_sends, ag_recvs)
    share_middle(groups, inners, 2, terms_a, land_a, stage_a, final_a)
    axis_start(groups, inners, "inner", stage_a, final_a, ai_sends, ai_recvs)
    exchange_wait(groups, inners, outbound, received, r_sends, r_recvs)

    layer_sum[...] = jnp.zeros_like(layer_sum)
    hidden_sums[3:4] = jnp.zeros((1, hidden), jnp.float32)

    def layer_step(step, carry):
        rows = pl.ds(pl.multiple_of(step * block, block), block)
        chosen = hot(iota(block, slots, 0) + step * block == lists_row[...])
        sums = dot_plain(chosen, received[...].reshape(slots, width))
        acts = pre_act[rows]
        s_act = sigmoid(acts)
        d_pre = sums * (s_act * (1.0 + acts * (1.0 - s_act)))
        low = d_pre.astype(LOW)
        d_pre_low[rows] = low
        hidden_sums[3:4, :width] += jnp.sum(d_pre, axis=0, keepdims=True)
        layer_sum[:width] += dot_first(x_self[rows], low)
        layer_sum[width:] += dot_first(x_agg[rows], low)
        return carry

    lax.fori_loop(0, nodes // block, layer_step, 0)
    layer_chunk = layer_sum.shape[0] // groups
    for index in range(groups):
        part = layer_sum[index * layer_chunk : (index + 1) * layer_chunk]
        terms_b[index] = (part / pairs).astype(LOW)
    bias[...] = jnp.zeros_like(bias)
    line = 0
    for row, span in ((0, hidden), (1, hidden), (2, hidden), (3, width)):
        for piece in range(span // 128):
            values = hidden_sums[row : row + 1, piece * 128 : (piece + 1) * 128]
            bias[line : line + 1] = values / pairs
            line += 1
    axis_start(groups, inners, "group", terms_b, land_b, bg_sends, bg_recvs)
    axis_start(groups, inners, "group", bias, bias_land, cg_sends, cg_recvs, True)
    axis_wait(groups, inners, "group", terms_b, land_b, bg_sends, bg_recvs)
    share_middle(groups, inners, 1, terms_b, land_b, stage_b, final_b)
    axis_start(groups, inners, "inner", stage_b, final_b, bi_sends, bi_recvs)
    axis_wait(groups, inners, "group", bias, bias_land, cg_sends, cg_recvs, True)
    bias_land[group] = bias[...]
    bias_stage[...] = sum_slots(groups, bias_land)
    bias_final[inner] = bias_stage[...]
    axis_start(groups, inners, "inner", bias_stage, bias_final, ci_sends, ci_recvs, True)
    axis_wait(groups, inners, "inner", stage_a, final_a, ai_sends, ai_recvs)
    total = sum_slots(inners, final_a)
    rows = chunk // inners
    half = hidden // 2
    scorer_share[:, :half] = total[:rows]
    scorer_share[:, half:] = total[rows : 2 * rows]
    axis_wait(groups, inners, "inner", stage_b, final_b, bi_sends, bi_recvs)
    layer_share[...] = sum_slots(inners, final_b)[: layer_chunk // inners]
    axis_wait(groups, inners, "inner", bias_stage, bias_final, ci_sends, ci_recvs, True)
    bias_out[...] = sum_slots(inners, bias_final)


def end_kernel(
    d_pre_low,
    w_self,
    w_nbr,
    scorer_share,
    layer_share,
    bias,
    grad_self,
    grad_agg,
    scorer_flat,
    layer_flat,
    bias_flat,
):
    grad_self[...] = dot_last(d_pre_low[...], w_self[...]).astype(LOW)
    grad_agg[...] = dot_last(d_pre_low[...], w_nbr[...]).astype(LOW)
    for share, flat in ((scorer_share, scorer_flat), (layer_share, layer_flat)):
        rows, width = share.shape
        lines = width // 128
        for line in range(lines):
            flat[pl.ds(line, rows, stride=lines)] = share[:, line * 128 : (line + 1) * 128]
    for line in range(bias_flat.shape[0] // 128):
        bias_flat[line * 128 : (line + 1) * 128] = bias[line]


def up_to(count, step):
    return -(-count // step) * step


def body(
    x_self,
    x_agg,
    w_self,
    w_nbr,
    b_layer,
    w_one,
    b_one,
    w_two,
    b_two,
    w_out,
    send_lists,
    endpoint_slots,
    neg_index,
):
    groups = lax.axis_size("group")
    inners = lax.axis_size("inner")
    owners = groups * inners
    nodes, width = x_self.shape
    hidden = w_two.shape[0]
    pos = endpoint_slots.shape[0]
    negatives = neg_index.shape[1]
    capacity = send_lists.shape[2]
    padded = up_to(capacity, 16)
    slots = owners * padded
    block = min(512, pos)
    blocks = pos * (1 + negatives) // block
    lists = send_lists.reshape(owners, capacity)
    ends = endpoint_slots.T
    negs = neg_index.T
    if padded != capacity:
        lists = jnp.pad(lists, ((0, 0), (0, padded - capacity)), constant_values=-1)
        ends = ends + (ends // capacity) * (padded - capacity)

    def f32(*shape):
        return VMEM(shape, jnp.float32)

    def low(*shape):
        return VMEM(shape, LOW)

    chunk_a = (width + hidden) // groups
    chunk_b = 2 * width // groups
    slab_a = up_to(2 * chunk_a // inners, 16)
    slab_b = up_to(chunk_b // inners, 16)
    lines = up_to((3 * hidden + width) // 128, 8)
    scratch = [
        f32(nodes, width),
        low(nodes, width),
        low(owners, padded, width),
        low(owners, padded, width),
        low(owners, padded, width),
        low(owners, padded, width),
        low(2 * pos, width),
        f32(2 * pos, width),
        low(2 * pos, width),
        low(blocks, block, width),
        low(blocks, block, hidden),
        low(blocks, block, hidden),
        low(blocks, block, hidden),
        f32(width + hidden, hidden),
        f32(8, hidden),
        f32(2 * width, width),
        low(groups, chunk_a, hidden),
        low(groups, chunk_a, hidden),
        low(inners, slab_a, hidden // 2),
        low(inners, slab_a, hidden // 2),
        low(groups, chunk_b, width),
        low(groups, chunk_b, width),
        low(inners, slab_b, width),
        low(inners, slab_b, width),
        f32(lines, 128),
        f32(groups, lines, 128),
        f32(lines, 128),
        f32(inners, lines, 128),
        f32(up_to(owners, 128), up_to(padded, 128)),
        f32(up_to(padded, 128), up_to(owners, 128)),
        VMEM((1, slots), jnp.int32),
        f32(128, pos),
        f32(pos, 128),
        VMEM((1, 2 * pos), jnp.int32),
    ]
    counts = [owners] * 4 + ([groups] * 2 + [inners] * 2) * 3
    flops = 2 * (pos * (1 + negatives) * 3 * hidden * (width + hidden))
    d_pre_low, scorer_share, layer_share, total = pl.pallas_call(
        functools.partial(kernel, groups, inners, block),
        out_shape=(
            jax.ShapeDtypeStruct((nodes, width), LOW),
            jax.ShapeDtypeStruct((chunk_a // inners, hidden), jnp.float32),
            jax.ShapeDtypeStruct((chunk_b // inners, width), jnp.float32),
            jax.ShapeDtypeStruct((lines, 128), jnp.float32),
        ),
        in_specs=[pl.BlockSpec(memory_space=VMEM)] * 13,
        out_specs=(pl.BlockSpec(memory_space=VMEM),) * 4,
        scratch_shapes=scratch + [pltpu.SemaphoreType.DMA((count,)) for count in counts],
        compiler_params=pltpu.CompilerParams(
            collective_id=0, has_side_effects=True, vmem_limit_bytes=56 * 1024 * 1024
        ),
        cost_estimate=pl.CostEstimate(flops=flops, bytes_accessed=2**23, transcendentals=2**22),
        name="link_backward",
    )(
        x_self,
        x_agg,
        w_self,
        w_nbr,
        b_layer[None],
        w_one,
        b_one[None],
        w_two,
        b_two[None],
        w_out[None],
        lists,
        ends,
        negs,
    )
    share_a, share_b = scorer_share.size, layer_share.size
    grad_self, grad_agg, scorer_flat, layer_flat, bias_total = pl.pallas_call(
        end_kernel,
        out_shape=(
            jax.ShapeDtypeStruct((nodes, width), LOW),
            jax.ShapeDtypeStruct((nodes, width), LOW),
            jax.ShapeDtypeStruct((share_a // 128, 128), jnp.float32),
            jax.ShapeDtypeStruct((share_b // 128, 128), jnp.float32),
            jax.ShapeDtypeStruct((3 * hidden + width,), jnp.float32),
        ),
        in_specs=[pl.BlockSpec(memory_space=VMEM)] * 6,
        out_specs=(pl.BlockSpec(memory_space=VMEM),) * 5,
        compiler_params=pltpu.CompilerParams(vmem_limit_bytes=60 * 1024 * 1024),
        name="end_products",
    )(d_pre_low, w_self, w_nbr, scorer_share, layer_share, total)
    return (grad_self, grad_agg, scorer_flat.reshape(-1), layer_flat.reshape(-1), bias_total)


def solution(mesh):
    rows = P(("group", "inner"), None)
    flat = P(("group", "inner"))
    return jax.shard_map(
        body,
        mesh=mesh,
        in_specs=(rows, rows) + (P(),) * 8 + (P(("group", "inner"), None, None), rows, rows),
        out_specs=(rows, rows, flat, flat, P()),
        check_vma=False,
    )
```
